32 devices in a mesh: seq: 16 (over z, y, core), ch: 2 (over x).
Axes of the slice: x: 2, y: 2, z: 4, core: 2. Of those that a mesh axis runs over, the one named last changes fastest.
Arguments:
- inputs: bfloat16 [262144, 2048], P('seq', 'ch'), may hold values from -6 to 6
- first_factor: bfloat16 [512, 512], P('ch'), may hold values from -0.25 to 0.25
- twiddle: float32 [512, 512], P('seq'), may hold values from -4 to 4
- second_factor: bfloat16 [512, 512], P('ch'), may hold values from -0.25 to 0.25
- block_first: bfloat16 [64, 32, 32], P('ch'), may hold values from -1 to 1
- block_second: bfloat16 [32, 64, 64], P('ch'), may hold values from -0.75 to 0.75
Outputs:
- mixed_out: bfloat16 [262144, 2048], P('seq', 'ch')
The draws below stay inside these ranges and needn't reach their ends.
All inputs are finite; a program needn't handle non-finite values.
Results may differ from the reference program's by a relative error of at most 0.007.
Values may be sent and summed in bfloat16 or wider, within the bound.
A program may use at most 576 MiB of HBM per device.

```python
import jax
import jax.numpy as jnp
from jax import lax

BLOCK = 512
CB1 = 64
CB2 = 32
D = 2048
L = 262144


def levels(rng, dims, split, smallest, high):
    level = 1.0
    for dim, shards_of in split:
        steps = jax.random.uniform(jax.random.fold_in(jax.random.fold_in(rng, 6), dim), (shards_of,), jnp.float32, smallest / len(split), high / len(split))
        level = level * jnp.repeat(jnp.exp(steps), dims[dim] // shards_of).reshape((-1,) + (1,) * (len(dims) - 1 - dim))
    return level


def centred(stream_key, dims, spread, reach, pieces=(), held_as=jnp.bfloat16):
    values = jax.random.normal(stream_key, dims, jnp.float32) * spread
    if len(pieces) > 0:
        values = levels(stream_key, dims, pieces, -0.22, 0.18) * values
    return jnp.clip(values, min=-reach, max=reach).astype(held_as)


def setup_inputs(seed: int = 0) -> dict:
    arg_keys = jax.random.split(jax.random.key(seed), 7)
    inputs = centred(arg_keys[0], (L, D), 1.0, 6.0, ((0, 16), (1, 2)))
    first_factor = centred(arg_keys[1], (BLOCK, BLOCK), BLOCK ** -0.5, 0.25, ((0, 2),))
    twiddle = centred(arg_keys[2], (BLOCK, BLOCK), 1.0, 4.0, ((0, 16),), jnp.float32)
    second_factor = centred(arg_keys[3], (BLOCK, BLOCK), BLOCK ** -0.5, 0.25, ((0, 2),))
    block_first = centred(arg_keys[4], (CB1, CB2, CB2), CB2 ** -0.5, 1.0, ((0, 2),))
    block_second = centred(arg_keys[5], (CB2, CB1, CB1), CB1 ** -0.5, 0.75, ((0, 2),))
    return {"inputs": inputs, "first_factor": first_factor, "twiddle": twiddle, "second_factor": second_factor, "block_first": block_first, "block_second": block_second}


def reference(inputs, first_factor, twiddle, second_factor, block_first, block_second):
    seq_grid = inputs.reshape(BLOCK, BLOCK, D)
    first_f32 = first_factor.astype(jnp.float32)
    second_f32 = second_factor.astype(jnp.float32)

    def group_mix(group_id):
        offset = (group_id * CB2).astype(jnp.int32)
        columns = lax.dynamic_slice_in_dim(seq_grid, offset, CB2, 2).astype(jnp.float32)
        first = jnp.einsum('kj,ijc->ikc', first_f32, columns)
        twisted = (first * twiddle[:, :, None]).astype(jnp.bfloat16)
        twisted = lax.optimization_barrier(twisted).astype(jnp.float32)
        second = jnp.einsum('pi,ikc->pkc', second_f32, twisted).astype(jnp.bfloat16)
        second = lax.optimization_barrier(second).astype(jnp.float32)
        return (columns * second).astype(jnp.bfloat16)

    stacked = lax.map(group_mix, jnp.arange(D // CB2, dtype=jnp.int32))
    gated = jnp.moveaxis(stacked, 0, 2).reshape(L, D)
    first_blocks = block_first.astype(jnp.float32)
    second_blocks = block_second.astype(jnp.float32)

    def channel_rows(row_id):
        offset = (row_id * BLOCK).astype(jnp.int32)
        rows_now = lax.dynamic_slice_in_dim(gated, offset, BLOCK, 0)
        grouped = rows_now.reshape(BLOCK, CB1, CB2).astype(jnp.float32)
        middle = jnp.einsum('amb,tab->tam', first_blocks, grouped).astype(jnp.bfloat16)
        middle = lax.optimization_barrier(middle).astype(jnp.float32)
        result_rows = jnp.einsum('mpa,tam->tmp', second_blocks, middle)
        return result_rows.reshape(BLOCK, D).astype(jnp.bfloat16)

    outputs = lax.map(channel_rows, jnp.arange(L // BLOCK, dtype=jnp.int32))
    return outputs.reshape(L, D)
```

```python
import jax
import jax.numpy as jnp
from jax import lax
from jax.sharding import PartitionSpec as P

BLOCK = 512
CHUNKS = 4


def local(inputs, first_factor, twiddle, second_factor, block_first, block_second):
    tok_rows, channels = inputs.shape
    outer_rows = tok_rows // BLOCK
    n_ch = lax.axis_size("ch")
    me = lax.axis_index("ch")
    a_loc, m_all, b_all = block_first.shape
    m_loc, p_all, a_all = block_second.shape
    token_grid = inputs.reshape(outer_rows, BLOCK, channels)
    contract = (((1,), (1,)), ((), ()))
    full_first = lax.all_gather(first_factor, "ch", axis=0, tiled=True)
    full_second = lax.all_gather(second_factor, "ch", axis=0, tiled=True)
    twiddle_t = jnp.transpose(twiddle)
    k_sub = BLOCK // CHUNKS

    eye_a = jnp.eye(a_loc, dtype=jnp.bfloat16)
    eye_m = jnp.eye(m_loc, dtype=jnp.bfloat16)
    first_dense, second_dense = [], []
    for shift in range(n_ch):
        to = lax.rem(me + shift, n_ch)
        source = lax.rem(me + n_ch - shift, n_ch)
        piece = lax.dynamic_slice_in_dim(block_first, to * m_loc, m_loc, 1)
        piece = jnp.transpose(piece, (0, 2, 1))[:, :, :, None] * eye_a[:, None, None, :]
        first_dense.append(piece.reshape(a_loc * b_all, m_loc * a_loc))
        piece = lax.dynamic_slice_in_dim(block_second, source * a_loc, a_loc, 2)
        piece = jnp.transpose(piece, (0, 2, 1))[:, :, None, :] * eye_m[:, None, :, None]
        second_dense.append(piece.reshape(m_loc * a_loc, m_loc * p_all))

    sent = []
    for q in range(CHUNKS):
        ks = slice(q * k_sub, (q + 1) * k_sub)
        first = lax.dot_general(
            full_first[ks], token_grid, contract, preferred_element_type=jnp.float32
        )
        twisted = (first * twiddle_t[ks][:, :, None]).astype(jnp.bfloat16)
        if q >= 2:
            twisted, sent[q - 2] = lax.optimization_barrier((twisted, sent[q - 2]))
        sent.append(lax.all_to_all(twisted, "seq", split_axis=0, concat_axis=1, tiled=True))

    by_owner = full_second.reshape(BLOCK // outer_rows, outer_rows, BLOCK)
    half = outer_rows // 2
    steps = [(q, 0, outer_rows) for q in range(CHUNKS - 1)]
    steps += [(CHUNKS - 1, 0, half), (CHUNKS - 1, half, outer_rows - half)]
    results, received = [], []
    for n, (q, low, rows) in enumerate(steps):
        ks = slice(q * k_sub, (q + 1) * k_sub)
        factor = by_owner[:, low : low + rows].reshape(-1, BLOCK)
        second = lax.dot_general(
            factor, sent[q], contract, preferred_element_type=jnp.float32
        ).astype(jnp.bfloat16)
        if n >= 2:
            second, received[n - 2] = lax.optimization_barrier((second, received[n - 2]))
        returned = lax.all_to_all(second, "seq", split_axis=0, concat_axis=1, tiled=True)
        gated = (
            token_grid[low : low + rows, ks].astype(jnp.float32)
            * returned.astype(jnp.float32)
        ).astype(jnp.bfloat16)
        gated = gated.reshape(rows * k_sub, channels)
        parts = []
        for shift in range(n_ch):
            middle = jnp.dot(
                gated, first_dense[shift], preferred_element_type=jnp.float32
            ).astype(jnp.bfloat16)
            if shift:
                middle = lax.ppermute(
                    middle, "ch", [(d, (d + shift) % n_ch) for d in range(n_ch)]
                )
            parts.append(middle)
        received.append(parts)
    for n, (q, low, rows) in enumerate(steps):
        total = None
        for shift in range(n_ch):
            term = jnp.dot(
                received[n][shift], second_dense[shift], preferred_element_type=jnp.float32
            )
            total = term if total is None else total + term
        results.append(total.astype(jnp.bfloat16).reshape(rows, k_sub, channels))
    results[-2:] = [jnp.concatenate(results[-2:], axis=0)]
    return jnp.concatenate(results, axis=1).reshape(tok_rows, channels)


def solution(mesh):
    placed = (
        P("seq", "ch"),
        P("ch", None),
        P("seq", None),
        P("ch", None),
        P("ch", None, None),
        P("ch", None, None),
    )
    return jax.shard_map(
        local, mesh=mesh, in_specs=placed, out_specs=P("seq", "ch"), check_vma=False
    )
```

```python
import jax
import jax.numpy as jnp
from jax import lax
from jax.sharding import PartitionSpec as P

BLOCK = 512
CHUNKS = 4


def local(inputs, first_factor, twiddle, second_factor, block_first, block_second):
    tok_rows, channels = inputs.shape
    outer_rows = tok_rows // BLOCK
    n_ch = lax.axis_size("ch")
    me = lax.axis_index("ch")
    a_loc, m_all, b_all = block_first.shape
    m_loc, p_all, a_all = block_second.shape
    token_grid = inputs.reshape(outer_rows, BLOCK, channels)
    contract = (((1,), (1,)), ((), ()))
    full_first = lax.all_gather(first_factor, "ch", axis=0, tiled=True)
    full_second = lax.all_gather(second_factor, "ch", axis=0, tiled=True)
    twiddle_t = jnp.transpose(twiddle)
    k_sub = BLOCK // CHUNKS

    eye_a = jnp.eye(a_loc, dtype=jnp.bfloat16)
    eye_m = jnp.eye(m_loc, dtype=jnp.bfloat16)
    first_dense, second_dense = [], []
    for shift in range(n_ch):
        to = lax.rem(me + shift, n_ch)
        source = lax.rem(me + n_ch - shift, n_ch)
        piece = lax.dynamic_slice_in_dim(block_first, to * m_loc, m_loc, 1)
        piece = jnp.transpose(piece, (0, 2, 1))[:, :, :, None] * eye_a[:, None, None, :]
        first_dense.append(piece.reshape(a_loc * b_all, m_loc * a_loc))
        piece = lax.dynamic_slice_in_dim(block_second, source * a_loc, a_loc, 2)
        piece = jnp.transpose(piece, (0, 2, 1))[:, :, None, :] * eye_m[:, None, :, None]
        second_dense.append(piece.reshape(m_loc * a_loc, m_loc * p_all))

    sent = []
    for q in range(CHUNKS):
        ks = slice(q * k_sub, (q + 1) * k_sub)
        first = lax.dot_general(
            full_first[ks], token_grid, contract, preferred_element_type=jnp.float32
        )
        twisted = (first * twiddle_t[ks][:, :, None]).astype(jnp.bfloat16)
        if q >= 2:
            twisted, sent[q - 2] = lax.optimization_barrier((twisted, sent[q - 2]))
        sent.append(lax.all_to_all(twisted, "seq", split_axis=0, concat_axis=1, tiled=True))

    by_owner = full_second.reshape(BLOCK // outer_rows, outer_rows, BLOCK)
    half, quarter = outer_rows // 2, outer_rows // 4
    steps = [(q, 0, outer_rows) for q in range(CHUNKS - 1)]
    steps += [
        (CHUNKS - 1, 0, half),
        (CHUNKS - 1, half, quarter),
        (CHUNKS - 1, half + quarter, outer_rows - half - quarter),
    ]

    def mix(n):
        q, low, rows = steps[n]
        factor = by_owner[:, low : low + rows].reshape(-1, BLOCK)
        return lax.dot_general(
            factor, sent[q], contract, preferred_element_type=jnp.float32
        ).astype(jnp.bfloat16)

    received = []
    second = mix(0)
    for n, (q, low, rows) in enumerate(steps):
        ks = slice(q * k_sub, (q + 1) * k_sub)
        after = None
        if n + 1 < len(steps):
            after = mix(n + 1)
            second, after = lax.optimization_barrier((second, after))
        ended = n - 2 if rows == outer_rows or low == 0 else n - 3
        if ended >= 0:
            second, received[ended] = lax.optimization_barrier((second, received[ended]))
        returned = lax.all_to_all(
            second.reshape(-1, rows, *second.shape[1:]), "seq", split_axis=0, concat_axis=0
        )
        second = after
        if n >= 1:
            returned, received[n - 1][0] = lax.optimization_barrier(
                (returned, received[n - 1][0])
            )
        returned = jnp.transpose(returned, (1, 0, 2, 3)).reshape(rows, k_sub, channels)
        gated = (
            token_grid[low : low + rows, ks].astype(jnp.float32)
            * returned.astype(jnp.float32)
        ).astype(jnp.bfloat16)
        gated = gated.reshape(rows * k_sub, channels)
        parts = []
        for shift in range(n_ch):
            middle = jnp.dot(
                gated, first_dense[shift], preferred_element_type=jnp.float32
            ).astype(jnp.bfloat16)
            if shift:
                middle = lax.ppermute(
                    middle, "ch", [(d, (d + shift) % n_ch) for d in range(n_ch)]
                )
            parts.append(middle)
        received.append(parts)

    result = jnp.zeros((outer_rows, BLOCK, channels), jnp.bfloat16)
    for n, (q, low, rows) in enumerate(steps):
        total = None
        for shift in range(n_ch):
            term = jnp.dot(
                received[n][shift], second_dense[shift], preferred_element_type=jnp.float32
            )
            total = term if total is None else total + term
        part = total.astype(jnp.bfloat16).reshape(rows, k_sub, channels)
        result = lax.dynamic_update_slice(result, part, (low, q * k_sub, 0))
    return result.reshape(tok_rows, channels)


def solution(mesh):
    placed = (
        P("seq", "ch"),
        P("ch", None),
        P("seq", None),
        P("ch", None),
        P("ch", None, None),
        P("ch", None, None),
    )
    return jax.shard_map(
        local, mesh=mesh, in_specs=placed, out_specs=P("seq", "ch"), check_vma=False
    )
```
